32 devices in a mesh: dp: 16 (over z, y, core), tensor: 2 (over x).
Axes of the slice: x: 2, y: 2, z: 4, core: 2. Of those that a mesh axis runs over, the one named last changes fastest.
Arguments:
- activations: bfloat16 [512, 16384], P('dp', 'tensor'), may hold values from -6 to 6
- weight: bfloat16 [16384, 16384], P('tensor', 'dp'), may hold values from -0.046875 to 0.046875
- out_grad: bfloat16 [512, 16384], P('tensor', 'dp'), may hold values from -6 to 6
Outputs:
- outputs: bfloat16 [512, 16384], P('tensor', 'dp')
- in_grad: bfloat16 [512, 16384], P('dp', 'tensor')
- weight_grad: float32 [16384, 16384], P('tensor', 'dp')
The draws below stay inside these ranges and needn't reach their ends.
All inputs are finite; a program needn't handle non-finite values.
Results may differ from the reference program's by a relative error of at most 0.0049.
Values may be sent and summed in bfloat16 or wider, within the bound.
No kernel may reach another device: no remote copies, remote signals or barrier semaphores. Data moves between devices by JAX's collectives and lax.ppermute only.
A program may use at most 128 MiB of HBM per device.

```python
import math
import jax
import jax.numpy as jnp
from jax import lax

D = 16384
F = 16384
TOKENS = 512


def level_of(rng, dims, split, low, largest):
    def one(dim, parts):
        steps = jax.random.uniform(jax.random.fold_in(jax.random.fold_in(rng, 6), dim), (parts,), jnp.float32, low / len(split), largest / len(split))
        return jnp.repeat(jnp.exp(steps), dims[dim] // parts).reshape((-1,) + (1,) * (len(dims) - dim - 1))

    factor_of = one(*split[0])
    for cut in split[1:]:
        factor_of = factor_of * one(*cut)
    return factor_of


def noise(key, extent, scale, most, cuts=(), held_as=jnp.bfloat16):
    drawn = jax.random.normal(key, extent, jnp.float32) * scale
    if len(cuts) > 0:
        drawn = level_of(key, extent, cuts, -0.22, 0.18) * drawn
    return jnp.clip(drawn, min=-most, max=most).astype(held_as)


def setup_inputs(seed: int = 0) -> dict:
    seeds = jax.random.split(jax.random.key(seed), 4)
    return {
        "activations": noise(seeds[0], (TOKENS, D), 1.0, 6.0, ((0, 16), (1, 2))),
        "weight": noise(seeds[1], (D, F), D ** -0.5, 0.046875, ((0, 2), (1, 16))),
        "out_grad": noise(seeds[2], (TOKENS, F), 1.0, 6.0, ((0, 2), (1, 16))),
    }


def signs_table(width):
    position = jnp.arange(width, dtype=jnp.int32)
    joined = jnp.bitwise_and(position[:, None], position[None, :])
    parity = jnp.zeros_like(joined)
    for bit_number in range(width.bit_length() - 1):
        parity = parity + jnp.bitwise_and(jnp.right_shift(joined, bit_number), 1)
    return jnp.where(parity % 2 == 1, -1.0, 1.0).astype(jnp.float32)

def transform(values, width):
    bit_count = width.bit_length() - 1
    first_size = 2 ** (bit_count // 2)
    second = width // first_size
    shaped = values.reshape(values.shape[0], first_size, second)
    result = jnp.einsum('rab,ac->rcb', shaped, signs_table(first_size), precision=lax.Precision.HIGHEST)
    result = jnp.einsum('rcb,bd->rcd', result, signs_table(second), precision=lax.Precision.HIGHEST)
    return result.reshape(values.shape[0], width)

def reference(activations, weight, out_grad):
    factor = 1.0 / math.sqrt(D)
    rotated = (transform(activations.astype(jnp.float32), D) * factor).astype(jnp.bfloat16)
    outputs = jnp.dot(rotated, weight, preferred_element_type=jnp.float32).astype(jnp.bfloat16)
    weight_grad = lax.dot_general(rotated, out_grad, (((0,), (0,)), ((), ())), preferred_element_type=jnp.float32) * (1.0 / math.sqrt(TOKENS))
    rotated_grad = lax.dot_general(out_grad, weight, (((1,), (1,)), ((), ())), preferred_element_type=jnp.float32)
    in_grad = (transform(rotated_grad, D) * factor).astype(jnp.bfloat16)
    return (outputs, in_grad, weight_grad)
```

```python
import functools
import math

import jax
import jax.numpy as jnp
from jax import lax
from jax.experimental import pallas as pl
from jax.experimental.pallas import tpu as pltpu
from jax.sharding import PartitionSpec as P

BF16 = jnp.bfloat16
F32 = jnp.float32
VMEM_LIMIT = 48 * 1024 * 1024


def swap(values, axis, mask):
    return lax.ppermute(values, axis, [(i, i ^ mask) for i in range(lax.axis_size(axis))])


def bit(number, place):
    return jnp.bitwise_and(jnp.right_shift(number, place), 1) == 1


def signs_table(width):
    position = jnp.arange(width, dtype=jnp.int32)
    joined = jnp.bitwise_and(position[:, None], position[None, :])
    parity = jnp.zeros_like(joined)
    for bit_number in range(width.bit_length() - 1):
        parity = parity + jnp.bitwise_and(jnp.right_shift(joined, bit_number), 1)
    return jnp.where(parity % 2 == 1, -1.0, 1.0).astype(F32)


def transform(values, width):
    bit_count = width.bit_length() - 1
    first_size = 2 ** (bit_count // 2)
    second = width // first_size
    shaped = values.reshape(values.shape[0], first_size, second)
    result = jnp.einsum(
        "rab,ac->rcb", shaped, signs_table(first_size), precision=lax.Precision.HIGHEST
    )
    result = jnp.einsum("rcb,bd->rcd", result, signs_table(second), precision=lax.Precision.HIGHEST)
    return result.reshape(values.shape[0], width)


def butterfly(values):
    position = lax.axis_index("tensor")
    result = values.astype(F32)
    for place in range(lax.axis_size("tensor").bit_length() - 1):
        other = swap(values.astype(BF16) if place == 0 else result, "tensor", 1 << place)
        other = other.astype(F32)
        result = jnp.where(bit(position, place), other - result, result + other)
    return result


def product_kernel(with_grad, with_out, has_sum, scale, *refs):
    refs = list(refs)
    even, odd = refs.pop(0), refs.pop(0)
    half = even.shape[0]
    if with_grad:
        cotangent = refs.pop(0)
    if with_out:
        weight = refs.pop(0)
    if has_sum:
        before = refs.pop(0)
    if with_grad:
        grad = refs[-2] if with_out else refs[-1]
        over_rows = (((0,), (0,)), ((), ()))
        total = lax.dot_general(
            even[...], cotangent[:half, :], over_rows, preferred_element_type=F32
        ) + lax.dot_general(odd[...], cotangent[half:, :], over_rows, preferred_element_type=F32)
        grad[...] = total * scale
    if with_out:
        out = refs[-1]

        @pl.when(pl.program_id(0) == 0)
        def _():
            out[...] = before[...] if has_sum else jnp.zeros_like(out)

        out[:half, :] += jnp.dot(even[...], weight[...], preferred_element_type=F32)
        out[half:, :] += jnp.dot(odd[...], weight[...], preferred_element_type=F32)


def product(even, odd, cotangent, weight, chunk, chunks, grad_before, sum_before, grad, out, scale):
    half, width = even.shape
    features, columns = weight.shape
    tile = min(512, width)
    steps = width // tile
    first = chunk * steps
    whole = lambda rows: pl.BlockSpec((rows, columns), lambda i: (0, 0))
    tall = pl.BlockSpec((tile, columns), lambda i: (first + i, 0))
    args, specs = [even, odd], [pl.BlockSpec((half, tile), lambda i: (0, i))] * 2
    aliases = {}
    if grad:
        args.append(cotangent)
        specs.append(whole(2 * half))
    if out:
        args.append(weight)
        specs.append(tall)
    if out and sum_before is not None:
        args.append(sum_before)
        specs.append(whole(2 * half))
    outs, out_specs = [], []
    if grad:
        if grad_before is not None:
            aliases[len(args)] = 0
            args.append(grad_before)
            specs.append(pl.BlockSpec(memory_space=pl.ANY))
        outs.append(jax.ShapeDtypeStruct((features, columns), F32))
        out_specs.append(tall)
    if out:
        outs.append(jax.ShapeDtypeStruct((2 * half, columns), F32))
        out_specs.append(whole(2 * half))
    kinds = int(grad) + int(out)
    return pl.pallas_call(
        functools.partial(product_kernel, grad, out, out and sum_before is not None, scale),
        grid=(steps,),
        in_specs=specs,
        out_specs=out_specs,
        out_shape=outs,
        input_output_aliases=aliases,
        compiler_params=pltpu.CompilerParams(vmem_limit_bytes=VMEM_LIMIT),
        cost_estimate=pl.CostEstimate(
            flops=kinds * 4 * half * width * columns,
            bytes_accessed=4 * half * width
            + (4 * width * columns if grad else 0)
            + (2 * width * columns if out else 0),
            transcendentals=0,
        ),
    )(*args)


def per_device(activations, weight, out_grad):
    dp, tensor = lax.axis_size("dp"), lax.axis_size("tensor")
    dp_bits, top_bits = dp.bit_length() - 1, tensor.bit_length() - 1
    low_bits = dp_bits - top_bits
    rows, width = activations.shape
    columns = weight.shape[1]
    me, mine = lax.axis_index("dp"), lax.axis_index("tensor")
    low_me = jnp.bitwise_and(me, (1 << low_bits) - 1)
    apart = jnp.bitwise_xor(jnp.right_shift(me, low_bits), mine)
    factor = 1.0 / math.sqrt(width * tensor)
    blocks = 1 << low_bits

    def reversed_bits(number):
        return sum((number >> b & 1) << (low_bits - 1 - b) for b in range(low_bits))

    def low_order(values, inverse=False):
        pieces = []
        for position in range(blocks):
            if inverse:
                source = sum(
                    jnp.bitwise_and(jnp.right_shift(jnp.bitwise_xor(low_me, position), b), 1)
                    << (low_bits - 1 - b)
                    for b in range(low_bits)
                )
            else:
                source = jnp.bitwise_xor(low_me, reversed_bits(position))
            pieces.append(lax.dynamic_slice_in_dim(values, source * rows, rows, 0))
        return jnp.concatenate(pieces, axis=0)

    def exchange_order(parts):
        for b in range(top_bits):
            flip = bit(apart, b)
            parts = [jnp.where(flip, parts[q ^ 1 << b], parts[q]) for q in range(tensor)]
        return parts

    rotated = (transform(butterfly(activations), width) * factor).astype(BF16)

    grads = [low_order(out_grad)]
    grads += [swap(grads[0], "tensor", q) for q in range(1, tensor)]

    sums = []
    for grad in grads:
        part = lax.dot_general(
            grad, weight, (((1,), (1,)), ((), ())), preferred_element_type=F32
        ).astype(BF16)
        part = part.reshape((2,) * low_bits + (rows, width))
        for place in range(low_bits):
            got = swap(part[1], "dp", 1 << place)
            part = part[0].astype(F32) + got.astype(F32)
            if place + 1 < low_bits:
                part = part.astype(BF16)
        sums.append(part)
    sums = exchange_order(sums)
    for place in reversed(range(top_bits)):
        count = 1 << place
        sums = [
            sums[j].astype(F32)
            + swap(sums[j + count].astype(BF16), "dp", count << low_bits).astype(F32)
            for j in range(count)
        ]
    rotated_grad = sums[0]

    ordered = exchange_order(grads)
    half = blocks * rows // 2
    cotangent = jnp.concatenate(
        [g[:half] for g in ordered] + [g[half:] for g in ordered], axis=0
    )
    chunks = 2
    chunk_width = width // chunks
    axes = [place for place in reversed(range(low_bits, dp_bits))] + list(range(1, low_bits))
    down = list(reversed(range(1, dp_bits)))
    up = list(reversed(range(low_bits, dp_bits))) + list(range(1, low_bits))
    grad_full, out_sum = None, None
    token_total = out_grad.shape[0] * tensor
    scale = 1.0 / math.sqrt(token_total)
    for chunk in range(chunks):
        got = rotated[:, chunk * chunk_width : (chunk + 1) * chunk_width]
        got = got.reshape((1,) * len(axes) + (rows, chunk_width))
        for place in down if chunk % 2 == 0 else up:
            got = jnp.concatenate([got, swap(got, "dp", 1 << place)], axis=axes.index(place))
        even = got.reshape(dp // 2 * rows, chunk_width)
        odd = swap(even, "dp", 1)
        call = functools.partial(
            product, even, odd, cotangent, weight, chunk, chunks, grad_full, out_sum, scale=scale
        )
        if chunk + 1 < chunks:
            grad_full, out_sum = call(grad=True, out=True)
        else:
            (out_sum,) = call(grad=False, out=True)
            (grad_full,) = call(grad=True, out=False)

    per_top = half
    parts = [
        jnp.concatenate(
            [
                out_sum[j * per_top : (j + 1) * per_top],
                out_sum[(tensor + j) * per_top : (tensor + j + 1) * per_top],
            ],
            axis=0,
        )
        for j in range(tensor)
    ]
    parts = exchange_order(parts)
    total = parts[0]
    for q in range(1, tensor):
        total = total + swap(parts[q].astype(BF16), "tensor", q).astype(F32)
    outputs = low_order(total.astype(BF16), inverse=True)

    in_grad = (transform(butterfly(rotated_grad), width) * factor).astype(BF16)
    return (outputs, in_grad, grad_full)


def solution(mesh):
    return jax.shard_map(
        per_device,
        mesh=mesh,
        in_specs=(P("dp", "tensor"), P("tensor", "dp"), P("tensor", "dp")),
        out_specs=(P("tensor", "dp"), P("dp", "tensor"), P("tensor", "dp")),
        check_vma=False,
    )
```

```python
import functools
import math

import jax
import jax.numpy as jnp
from jax import lax
from jax.experimental import pallas as pl
from jax.experimental.pallas import tpu as pltpu
from jax.sharding import PartitionSpec as P

BF16 = jnp.bfloat16
F32 = jnp.float32
VMEM_LIMIT = 60 * 1024 * 1024
VMEM_MOST = 63 * 1024 * 1024
LANES = 128


def swap(values, axis, mask):
    return lax.ppermute(values, axis, [(i, i ^ mask) for i in range(lax.axis_size(axis))])


def bit(number, place):
    return jnp.bitwise_and(jnp.right_shift(number, place), 1) == 1


def reversed_bits(number, count):
    return sum((number >> b & 1) << (count - 1 - b) for b in range(count))


def exchange_order(parts, apart):
    for b in range(len(parts).bit_length() - 1):
        flip = bit(apart, b)
        parts = [jnp.where(flip, parts[q ^ 1 << b], parts[q]) for q in range(len(parts))]
    return parts


class Chain:
    def __init__(self, place):
        self.place = place
        self.last = []

    def __call__(
        self,
        body,
        inputs,
        in_specs,
        outs,
        out_specs,
        steps=1,
        scratch=(),
        aliases=None,
        flops=0,
        limit=VMEM_LIMIT,
        late=(),
    ):
        count, extra = len(inputs), len(self.last)

        late = list(late)
        made = len(outs)
        skipped = count + len(late) + extra

        def kernel(place, *refs):
            body(
                place,
                *refs[:count],
                *refs[skipped : skipped + made],
                *refs[skipped + made + len(late) :],
            )

        moved = sum(math.prod(v.shape) * v.dtype.itemsize for v in list(inputs) + list(outs))
        result = pl.pallas_call(
            kernel,
            grid=(steps,),
            in_specs=[pl.BlockSpec(memory_space=pltpu.SMEM)]
            + list(in_specs)
            + [pl.BlockSpec(memory_space=pl.ANY)] * (len(late) + extra),
            out_specs=list(out_specs) + [pl.BlockSpec(memory_space=pl.ANY)] * len(late),
            scratch_shapes=list(scratch),
            out_shape=list(outs) + [jax.ShapeDtypeStruct(v.shape, v.dtype) for v in late],
            input_output_aliases={1 + k: v for k, v in (aliases or {}).items()}
            | {1 + count + k: made + k for k in range(len(late))},
            compiler_params=pltpu.CompilerParams(vmem_limit_bytes=limit),
            cost_estimate=pl.CostEstimate(flops=flops, bytes_accessed=moved, transcendentals=0),
        )(self.place, *inputs, *late, *self.last)
        self.last = [result[made - 1]]
        return result

    def gate(self, values, after):
        count = len(values)

        def body(*refs):
            del refs

        return pl.pallas_call(
            body,
            in_specs=[pl.BlockSpec(memory_space=pl.ANY)] * (count + len(after)),
            out_specs=[pl.BlockSpec(memory_space=pl.ANY)] * count,
            out_shape=[jax.ShapeDtypeStruct(v.shape, v.dtype) for v in values],
            input_output_aliases={k: k for k in range(count)},
        )(*values, *after)

    def follow(self, *values):
        self.last.extend(values)


def whole(shape):
    return pl.BlockSpec(shape, lambda i: (0,) * len(shape))


def across(rows, tile):
    return pl.BlockSpec((rows, tile), lambda i: (0, i))


def array(rows, columns, kind=BF16):
    return jax.ShapeDtypeStruct((rows, columns), kind)


def cotangent_product(chain, grad, weight, rows, low_bits, reorder, cuts=1, late=()):
    tokens, columns = grad.shape
    width = weight.shape[0]
    tile = min(2048, width)
    blocks = 1 << low_bits

    def body(place, grad, weight, *outs):
        if reorder:
            ordered = outs[-1]

            @pl.when(pl.program_id(0) == 0)
            def _():
                for position in range(blocks):
                    source = place[0] ^ reversed_bits(position, low_bits)
                    start = pl.multiple_of(source * rows, rows)
                    ordered[position * rows : (position + 1) * rows, :] = grad[
                        pl.ds(start, rows), :
                    ]

            grad = ordered
        result = lax.dot_general(
            grad[...], weight[...], (((1,), (1,)), ((), ())), preferred_element_type=F32
        ).astype(BF16)
        for position in range(plain):
            outs[position][...] = result[position * rows : (position + 1) * rows]
        for position in range(plain, blocks):
            for piece in range(cuts):
                out = outs[plain + (position - plain) * cuts + piece]

                @pl.when(pl.program_id(0) // each == piece)
                def _(out=out, position=position):
                    out[...] = result[position * rows : (position + 1) * rows]

    steps = width // tile
    cuts = min(cuts, steps)
    each = steps // cuts
    plain = blocks - blocks // 4
    count = plain + (blocks - plain) * cuts
    piece_specs = [
        pl.BlockSpec((rows, tile), lambda i, k=k: (0, jnp.clip(i - k * each, 0, each - 1)))
        for k in range(cuts)
    ]
    made = chain(
        body,
        [grad, weight],
        [whole((tokens, columns)), pl.BlockSpec((tile, columns), lambda i: (i, 0))],
        [array(rows, width)] * plain
        + [array(rows, width // cuts)] * (count - plain)
        + [array(tokens, columns)] * reorder,
        [across(rows, tile)] * plain
        + piece_specs * (blocks - plain)
        + [whole((tokens, columns))] * reorder,
        steps,
        flops=2 * tokens * width * columns,
        late=late,
    )
    pieces = [list(made[k : k + cuts]) for k in range(plain, count, cuts)]
    return list(made[:plain]) + pieces, list(made[count:])


def add(first, *others):
    total = first.astype(F32)
    for other in others:
        total = total + other.astype(F32)
    return total


def exchange_last(values):
    position = lax.axis_index("tensor")
    places = lax.axis_size("tensor").bit_length() - 1
    for place in range(places):
        sent = values.astype(BF16) if place == 0 else values
        other = swap(sent, "tensor", 1 << place)
        if place + 1 < places:
            own, other = values.astype(F32), other.astype(F32)
            values = jnp.where(bit(position, place), other - own, own + other)
    return values, other


def rotate(chain, pairs, places, factor, copies=1, sums=()):
    rows = pairs[0][0].shape[0]
    widths = [own.shape[1] for own, _ in pairs]
    width = sum(widths)
    blocks = width // LANES

    def body(place, *refs):
        ins, outs = refs[: 2 * len(pairs)], refs[len(flat) :]
        terms = list(refs[2 * len(pairs) : len(flat)])
        for k, (_, others) in enumerate(sums):
            own, start = terms.pop(0), 0
            for _ in others:
                other = terms.pop(0)
                there = slice(start, start + other.shape[1])
                total = own[:, there].astype(F32) + other[...].astype(F32)
                outs[-1][k * rows : (k + 1) * rows, there] = total.astype(BF16)
                start += other.shape[1]
        upper = bit(place[2], places - 1)
        columns = []
        for k in range(len(pairs)):
            own, other = ins[2 * k], ins[2 * k + 1]
            for start in range(0, widths[k], LANES):
                here = slice(start, start + LANES)
                a, b = own[:, here].astype(F32), other[:, here].astype(F32)
                columns.append(jnp.where(upper, b - a, a + b))
        values = jnp.concatenate(columns, axis=0)
        i = lax.broadcasted_iota(jnp.int32, (LANES, LANES), 0)
        j = lax.broadcasted_iota(jnp.int32, (LANES, LANES), 1)
        parity = i & j
        for shift in (4, 2, 1):
            parity = parity ^ (parity >> shift)
        signs = jnp.where(parity & 1 == 1, -1.0, 1.0).astype(BF16)
        high = values.astype(BF16)
        rest = values - high.astype(F32)
        middle = rest.astype(BF16)
        low = (rest - middle.astype(F32)).astype(BF16)
        result = (
            jnp.dot(low, signs, preferred_element_type=F32)
            + jnp.dot(middle, signs, preferred_element_type=F32)
        ) + jnp.dot(high, signs, preferred_element_type=F32)
        apart = 1
        while apart < blocks:
            shaped = result.reshape(blocks // (2 * apart), 2, apart * rows, LANES)
            a, b = shaped[:, 0], shaped[:, 1]
            result = jnp.stack([a + b, a - b], axis=1).reshape(blocks * rows, LANES)
            apart *= 2
        result = (result * factor).astype(BF16)
        for block in range(blocks):
            for copy in range(copies):
                outs[copy][:, block * LANES : (block + 1) * LANES] = result[
                    block * rows : (block + 1) * rows
                ]

    flat = [v for pair in pairs for v in pair]
    flat += [v for own, others in sums for v in [own] + list(others)]
    shapes = [(rows, width)] * copies + [(len(sums) * rows, width)] * (len(sums) > 0)
    return chain(
        body,
        flat,
        [whole(v.shape) for v in flat],
        [array(*shape) for shape in shapes],
        [whole(shape) for shape in shapes],
        flops=6 * rows * width * LANES,
    )


def product(
    chain,
    gathered,
    grads,
    weight,
    columns_from,
    width,
    inner,
    before=None,
    into=None,
    grad=False,
    out=0,
    last=False,
    late=(),
):
    features, columns = weight.shape
    tile = min(1024, width)
    steps = width // tile
    first = columns_from // tile
    count = len(grads)
    held = count * inner
    groups = len(gathered)
    flat = [v for group in gathered for v in group]
    tall = pl.BlockSpec((tile, columns), lambda i: (first + i, 0))
    share = whole((out * inner, columns))
    inputs = list(flat)
    specs = [
        across(v.shape[0], tile)
        if v.shape[1] == width
        else pl.BlockSpec((v.shape[0], tile), lambda i: (0, first + i))
        for v in flat
    ]
    outs, out_specs, scratch, aliases = [], [], [], {}
    if grad:
        inputs += grads
        specs += [whole(v.shape) for v in grads]
        outs.append(array(features, columns, F32))
        out_specs.append(tall)
        scratch.append(pltpu.VMEM((groups * held, columns), BF16))
    if out:
        square = whole((out * held, columns))
        inputs.append(weight)
        specs.append(tall)
        if before is not None:
            inputs.append(before)
            specs.append(square)
        if last:
            outs += [array(out * inner, columns, F32)] + [array(out * inner, columns)] * (count - 1)
            out_specs += [share] * count
            scratch.append(pltpu.VMEM((out * held, columns), F32))
        else:
            outs.append(array(out * held, columns, F32))
            out_specs.append(square)
    if into is not None:
        aliases[len(inputs)] = 0
        inputs.append(into)
        specs.append(pl.BlockSpec(memory_space=pl.ANY))

    def body(place, *refs):
        refs = list(refs)
        step = pl.program_id(0)
        held_rows = [refs.pop(0) for _ in flat]
        shares = [refs.pop(0) for _ in range(count)] if grad else []
        if out:
            weight = refs.pop(0)
            earlier = refs.pop(0) if before is not None else None
        if aliases:
            refs.pop(0)
        rotated = jnp.concatenate([v[...] for v in held_rows], axis=0)
        if grad:
            result = refs.pop(0)
            cotangent = refs.pop(-2 if out and last else -1)

            @pl.when(step == 0)
            def _():
                parts = exchange_order([s[...] for s in shares], place[1])
                for group in range(groups):
                    start = (group % 2 * 2 + group // 2) * inner
                    for j, part in enumerate(parts):
                        to = group * held + j * inner
                        cotangent[to : to + inner, :] = part[start : start + inner]

            result[...] = (
                lax.dot_general(
                    rotated, cotangent[...], (((0,), (0,)), ((), ())), preferred_element_type=F32
                )
                * chain.scale
            )
        if out:
            total = refs.pop(-1)

            @pl.when(step == 0)
            def _():
                total[...] = jnp.zeros_like(total) if earlier is None else earlier[...]

            total[...] += jnp.dot(
                rotated[(groups - out) * held :], weight[...], preferred_element_type=F32
            )
            if last:

                @pl.when(step == steps - 1)
                def _():
                    for side in range(out):
                        start = side * held
                        parts = [
                            total[start + j * inner : start + (j + 1) * inner, :]
                            for j in range(count)
                        ]
                        for ref, part in zip(refs, exchange_order(parts, place[1])):
                            ref[side * inner : (side + 1) * inner, :] = part.astype(ref.dtype)

    return chain(
        body,
        inputs,
        specs,
        outs,
        out_specs,
        steps,
        scratch,
        aliases,
        flops=2 * width * columns * held * (groups * grad + out),
        limit=VMEM_MOST,
        late=late,
    )


def finish(chain, shares, rows, low_bits):
    rest = 1 << (low_bits - 2)

    def body(place, *refs):
        *shares, out = refs
        for position in range(1 << low_bits):
            side, middle = position // (2 * rest), position // rest % 2
            start = ((middle * 2 + side) * rest + position % rest) * rows
            here = slice(start, start + rows)
            total = shares[0][here, :]
            for other in shares[1:]:
                total = total + other[here, :].astype(F32)
            target = place[0] ^ reversed_bits(position, low_bits)
            out[pl.ds(pl.multiple_of(target * rows, rows), rows), :] = total.astype(BF16)

    shape = shares[0].shape
    (out,) = chain(
        body, shares, [whole(shape)] * len(shares), [array(*shape)], [whole(shape)]
    )
    return out


def per_device(activations, weight, out_grad):
    dp, tensor = lax.axis_size("dp"), lax.axis_size("tensor")
    dp_bits, top_bits = dp.bit_length() - 1, tensor.bit_length() - 1
    low_bits = dp_bits - top_bits
    rows, width = activations.shape
    me, mine = lax.axis_index("dp"), lax.axis_index("tensor")
    low_me = jnp.bitwise_and(me, (1 << low_bits) - 1)
    apart = jnp.bitwise_xor(jnp.right_shift(me, low_bits), mine)
    chain = Chain(jnp.stack([low_me, apart, mine]).astype(jnp.int32))
    chain.scale = 1.0 / math.sqrt(out_grad.shape[0] * tensor)
    factor = 1.0 / math.sqrt(width * tensor)
    rest = 1 << (low_bits - 2)
    inner = rest * rows

    def near(values, p):
        return swap(values, "dp", 1 << p)

    def core_send(blocks):
        half = len(blocks) // 2
        return [
            [kept, [near(v, 0) for v in went] if isinstance(went, list) else near(went, 0)]
            for kept, went in zip(blocks[:half], blocks[half:])
        ]

    def split_send(terms, p, *more):
        half = len(terms) // 2
        message = jnp.concatenate([add(*t).astype(BF16) for t in terms[half:]] + list(more), axis=0)
        came = near(message, p)
        pieces = [came[k * rows : (k + 1) * rows] for k in range(half + len(more))]
        kept = [t + [piece] for t, piece in zip(terms[:half], pieces)]
        return kept, pieces[half:], message

    rotation = exchange_last(activations)
    own, (ordered,) = cotangent_product(
        chain, out_grad, weight, rows, low_bits, True, 2
    )
    own = core_send(own)
    far = [swap(ordered, "tensor", q) for q in range(1, tensor)]
    half = len(own) // 2
    sent, rotated, message = rotate(chain, [rotation], top_bits, factor, 2, own[half:])
    came = near(message, 1)
    own = [terms + [came[k * rows : (k + 1) * rows]] for k, terms in enumerate(own[:half])]

    wide = list(range(2, dp_bits))
    gathered = {0: sent}
    for p in reversed(wide):
        for j in list(gathered):
            if p > 2 or j == 0:
                gathered[j | 1 << p] = near(gathered[j], p)
    gathered[0] = rotated

    others = []
    for q, grad in enumerate(far):
        late = [terms[0] for terms in own] if q == 0 else []
        products, late = cotangent_product(
            chain, grad, weight, rows, low_bits, False, 1, late
        )
        if q == 0:
            own = [[first] + terms[1:] for first, terms in zip(late, own)]
        plain = [v[0] if isinstance(v, list) else v for v in products]
        others.append(core_send(plain))

    ahead = [j for j in gathered if j and j < 1 << dp_bits and not j & 4]
    if low_bits > 2:
        own, pieces, message = split_send(own, 2, *[gathered[j] for j in ahead])
    else:
        message = jnp.concatenate([gathered[j] for j in ahead], axis=0)
        came = near(message, 2)
        pieces = [came[k * rows : (k + 1) * rows] for k in range(len(ahead))]
    gathered.update({j | 4: piece for j, piece in zip(ahead, pieces)})
    for p in range(3, low_bits):
        own, _, message = split_send(own, p)

    def gate_first(parts, after):
        held = list(chain.gate([terms[0] for part in parts for terms in part], after))
        return [[[held.pop(0)] + terms[1:] for terms in part] for part in parts]

    others = gate_first(others, [message])
    others = [split_send(part, 1)[0] for part in others]

    order = [
        t << low_bits | reversed_bits(r, low_bits - 2) << 2
        for t in range(tensor)
        for r in range(rest)
    ]
    here = [gathered[j] for j in order]
    core = [near(block, 0) for block in here]
    cut = width * 5 // 8
    ranges = [(0, cut), (cut, width - cut)]
    across_sent = [
        jnp.concatenate([block[:, start : start + size] for block in here], axis=0)
        for start, size in ranges
    ]
    others = gate_first(others, across_sent[:1])
    messages = []
    for p in range(2, low_bits):
        sent_parts = [split_send(part, p) for part in others]
        others = [part for part, _, _ in sent_parts]
        messages = [message for _, _, message in sent_parts]
    chain.follow(across_sent[0], *messages)
    grads = [ordered] + far
    arrived = [near(across_sent[0], 1)]

    some = exchange_order([add(*part[0]) for part in [own] + others], apart)
    for p in reversed(range(top_bits)):
        count = 1 << p
        pairs = [
            (some[j], swap(some[j + count].astype(BF16), "dp", count << low_bits))
            for j in range(count)
        ]
        some = [add(*pair) for pair in pairs]
    kept, came = pairs[0]
    arrived.append(near(across_sent[1], 1))
    arrived_core = [near(arrived[0], 0)]
    start, size = ranges[0]
    weight_grad, total, kept = product(
        chain, [here, core, [arrived[0]], [arrived_core[0]]], grads, weight, start, size, inner,
        grad=True, out=4, late=[kept],
    )
    (arrived[1],) = chain.gate(arrived[1:], [total])
    arrived_core.append(near(arrived[1], 0))
    rotated_grad = add(kept, came)
    final = exchange_last(rotated_grad)
    chain.follow(rotated_grad)
    start, size = ranges[1]
    result = product(
        chain, [here, core, [arrived[1]], [arrived_core[1]]], grads, weight, start, size, inner,
        before=total, out=4, last=True,
    )
    shares = [result[0]] + [swap(result[q], "tensor", q) for q in range(1, tensor)]
    (in_grad,) = rotate(chain, [final], top_bits, factor)
    (weight_grad,) = product(
        chain, [here, core, [arrived[1]], [arrived_core[1]]], grads, weight, start, size, inner,
        into=weight_grad, grad=True,
    )
    outputs = finish(chain, shares, rows, low_bits)
    return (outputs, in_grad, weight_grad)


def solution(mesh):
    return jax.shard_map(
        per_device,
        mesh=mesh,
        in_specs=(P("dp", "tensor"), P("tensor", "dp"), P("tensor", "dp")),
        out_specs=(P("tensor", "dp"), P("dp", "tensor"), P("tensor", "dp")),
        check_vma=False,
    )
```

```python
import functools
import math

import jax
import jax.numpy as jnp
from jax import lax
from jax.experimental import pallas as pl
from jax.experimental.pallas import tpu as pltpu
from jax.sharding import PartitionSpec as P

BF16 = jnp.bfloat16
F32 = jnp.float32
VMEM_LIMIT = 67000000
LANES = 128


def swap(values, axis, mask):
    return lax.ppermute(values, axis, [(i, i ^ mask) for i in range(lax.axis_size(axis))])


def bit(number, place):
    return jnp.bitwise_and(jnp.right_shift(number, place), 1) == 1


def reversed_bits(number, count):
    return sum((number >> b & 1) << (count - 1 - b) for b in range(count))


def exchange_order(parts, apart):
    for b in range(len(parts).bit_length() - 1):
        flip = bit(apart, b)
        parts = [jnp.where(flip, parts[q ^ 1 << b], parts[q]) for q in range(len(parts))]
    return parts


class Chain:
    def __init__(self, place):
        self.place = place
        self.last = []

    def __call__(
        self,
        body,
        inputs,
        in_specs,
        outs,
        out_specs,
        steps=1,
        scratch=(),
        aliases=None,
        flops=0,
        late=(),
    ):
        count, extra = len(inputs), len(self.last)

        late = list(late)
        made = len(outs)
        skipped = count + len(late) + extra

        def kernel(place, *refs):
            body(
                place,
                *refs[:count],
                *refs[skipped : skipped + made],
                *refs[skipped + made + len(late) :],
            )

        moved = sum(math.prod(v.shape) * v.dtype.itemsize for v in list(inputs) + list(outs))
        result = pl.pallas_call(
            kernel,
            grid=(steps,),
            in_specs=[pl.BlockSpec(memory_space=pltpu.SMEM)]
            + list(in_specs)
            + [pl.BlockSpec(memory_space=pl.ANY)] * (len(late) + extra),
            out_specs=list(out_specs) + [pl.BlockSpec(memory_space=pl.ANY)] * len(late),
            scratch_shapes=list(scratch),
            out_shape=list(outs) + [jax.ShapeDtypeStruct(v.shape, v.dtype) for v in late],
            input_output_aliases={1 + k: v for k, v in (aliases or {}).items()}
            | {1 + count + k: made + k for k in range(len(late))},
            compiler_params=pltpu.CompilerParams(vmem_limit_bytes=VMEM_LIMIT),
            cost_estimate=pl.CostEstimate(flops=flops, bytes_accessed=moved, transcendentals=0),
        )(self.place, *inputs, *late, *self.last)
        self.last = [result[made - 1]]
        return result

    def gate(self, values, after):
        count = len(values)

        def body(*refs):
            del refs

        return pl.pallas_call(
            body,
            in_specs=[pl.BlockSpec(memory_space=pl.ANY)] * (count + len(after)),
            out_specs=[pl.BlockSpec(memory_space=pl.ANY)] * count,
            out_shape=[jax.ShapeDtypeStruct(v.shape, v.dtype) for v in values],
            input_output_aliases={k: k for k in range(count)},
        )(*values, *after)

    def follow(self, *values):
        self.last.extend(values)


def whole(shape):
    return pl.BlockSpec(shape, lambda i: (0,) * len(shape))


def across(rows, tile):
    return pl.BlockSpec((rows, tile), lambda i: (0, i))


def array(rows, columns, kind=BF16):
    return jax.ShapeDtypeStruct((rows, columns), kind)


def cotangent_product(chain, grad, weight, rows, low_bits, reorder, cuts=1, late=()):
    tokens, columns = grad.shape
    width = weight.shape[0]
    tile = min(2048, width)
    blocks = 1 << low_bits

    def body(place, grad, weight, *outs):
        if reorder:
            ordered = outs[-1]

            @pl.when(pl.program_id(0) == 0)
            def _():
                for position in range(blocks):
                    source = place[0] ^ reversed_bits(position, low_bits)
                    start = pl.multiple_of(source * rows, rows)
                    ordered[position * rows : (position + 1) * rows, :] = grad[
                        pl.ds(start, rows), :
                    ]

            grad = ordered
        result = lax.dot_general(
            grad[...], weight[...], (((1,), (1,)), ((), ())), preferred_element_type=F32
        ).astype(BF16)
        for position in range(plain):
            outs[position][...] = result[position * rows : (position + 1) * rows]
        for position in range(plain, blocks):
            for piece in range(cuts):
                out = outs[plain + (position - plain) * cuts + piece]

                @pl.when(pl.program_id(0) // each == piece)
                def _(out=out, position=position):
                    out[...] = result[position * rows : (position + 1) * rows]

    steps = width // tile
    cuts = min(cuts, steps)
    each = steps // cuts
    plain = blocks - blocks // 4
    count = plain + (blocks - plain) * cuts
    piece_specs = [
        pl.BlockSpec((rows, tile), lambda i, k=k: (0, jnp.clip(i - k * each, 0, each - 1)))
        for k in range(cuts)
    ]
    made = chain(
        body,
        [grad, weight],
        [whole((tokens, columns)), pl.BlockSpec((tile, columns), lambda i: (i, 0))],
        [array(rows, width)] * plain
        + [array(rows, width // cuts)] * (count - plain)
        + [array(tokens, columns)] * reorder,
        [across(rows, tile)] * plain
        + piece_specs * (blocks - plain)
        + [whole((tokens, columns))] * reorder,
        steps,
        flops=2 * tokens * width * columns,
        late=late,
    )
    pieces = [list(made[k : k + cuts]) for k in range(plain, count, cuts)]
    return list(made[:plain]) + pieces, list(made[count:])


def add(first, *others):
    total = first.astype(F32)
    for other in others:
        total = total + other.astype(F32)
    return total


def exchange_last(values):
    position = lax.axis_index("tensor")
    places = lax.axis_size("tensor").bit_length() - 1
    for place in range(places):
        sent = values.astype(BF16) if place == 0 else values
        other = swap(sent, "tensor", 1 << place)
        if place + 1 < places:
            own, other = values.astype(F32), other.astype(F32)
            values = jnp.where(bit(position, place), other - own, own + other)
    return values, other


def rotate(chain, pairs, places, factor, copies=1, sums=(), first=0):
    rows = pairs[0][0].shape[0]
    widths = [own.shape[1] for own, _ in pairs]
    width = sum(widths)
    blocks = width // LANES

    def body(place, *refs):
        ins, outs = refs[: 2 * len(pairs)], refs[len(flat) :]
        terms = list(refs[2 * len(pairs) : len(flat)])
        for k, (_, others) in enumerate(sums):
            own, start = terms.pop(0), 0
            for _ in others:
                other = terms.pop(0)
                there = slice(start, start + other.shape[1])
                total = own[:, there].astype(F32) + other[...].astype(F32)
                outs[copies][k * rows : (k + 1) * rows, there] = total.astype(BF16)
                start += other.shape[1]
        upper = bit(place[2], places - 1)
        columns = []
        for k in range(len(pairs)):
            own, other = ins[2 * k], ins[2 * k + 1]
            for start in range(0, widths[k], LANES):
                here = slice(start, start + LANES)
                a, b = own[:, here].astype(F32), other[:, here].astype(F32)
                columns.append(jnp.where(upper, b - a, a + b))
        values = jnp.concatenate(columns, axis=0)
        i = lax.broadcasted_iota(jnp.int32, (LANES, LANES), 0)
        j = lax.broadcasted_iota(jnp.int32, (LANES, LANES), 1)
        parity = i & j
        for shift in (4, 2, 1):
            parity = parity ^ (parity >> shift)
        signs = jnp.where(parity & 1 == 1, -1.0, 1.0).astype(BF16)
        high = values.astype(BF16)
        rest = values - high.astype(F32)
        middle = rest.astype(BF16)
        low = (rest - middle.astype(F32)).astype(BF16)
        result = (
            jnp.dot(low, signs, preferred_element_type=F32)
            + jnp.dot(middle, signs, preferred_element_type=F32)
        ) + jnp.dot(high, signs, preferred_element_type=F32)
        apart = 1
        while apart < blocks:
            shaped = result.reshape(blocks // (2 * apart), 2, apart * rows, LANES)
            a, b = shaped[:, 0], shaped[:, 1]
            result = jnp.stack([a + b, a - b], axis=1).reshape(blocks * rows, LANES)
            apart *= 2
        result = (result * factor).astype(BF16)
        for block in range(blocks):
            for copy in range(copies):
                outs[copy][:, block * LANES : (block + 1) * LANES] = result[
                    block * rows : (block + 1) * rows
                ]
            if block * LANES < first:
                outs[-1][:, block * LANES : (block + 1) * LANES] = result[
                    block * rows : (block + 1) * rows
                ]

    flat = [v for pair in pairs for v in pair]
    flat += [v for own, others in sums for v in [own] + list(others)]
    shapes = [(rows, width)] * copies + [(len(sums) * rows, width)] * (len(sums) > 0)
    shapes += [(rows, first)] * (first > 0)
    return chain(
        body,
        flat,
        [whole(v.shape) for v in flat],
        [array(*shape) for shape in shapes],
        [whole(shape) for shape in shapes],
        flops=6 * rows * width * LANES,
    )


def product(
    chain,
    gathered,
    grads,
    weight,
    columns_from,
    width,
    inner,
    before=None,
    into=None,
    grad=False,
    out=0,
    last=False,
    late=(),
    origin=None,
):
    features, columns = weight.shape
    origin = columns_from if origin is None else origin
    tile = math.gcd(1024, math.gcd(columns_from - origin, math.gcd(columns_from, width)))
    steps = width // tile
    first = columns_from // tile
    ahead = (columns_from - origin) // tile
    count = lax.axis_size("tensor")
    held = count * inner
    groups = len(gathered)
    flat = [v for group in gathered for v in group]
    tall = pl.BlockSpec((tile, columns), lambda i: (first + i, 0))
    share = whole((out * inner, columns))
    inputs = list(flat)
    specs = [
        pl.BlockSpec(
            (v.shape[0], tile),
            lambda i, skip=first if v.shape[1] == features else ahead: (0, skip + i),
        )
        for v in flat
    ]
    outs, out_specs, scratch, aliases = [], [], [], {}
    if grad:
        inputs += grads
        specs += [whole(v.shape) for v in grads]
        outs.append(array(features, columns, F32))
        out_specs.append(tall)
        scratch.append(pltpu.VMEM((groups * held, columns), BF16))
    if out:
        square = whole((out * held, columns))
        inputs.append(weight)
        specs.append(tall)
        if before is not None:
            inputs.append(before)
            specs.append(whole(before.shape))
        if last:
            outs += [array(out * inner, columns, F32)] + [array(out * inner, columns)] * (count - 1)
            out_specs += [share] * count
            scratch.append(pltpu.VMEM((out * held, columns), F32))
        else:
            outs.append(array(out * held, columns, F32))
            out_specs.append(square)
    if into is not None:
        aliases[len(inputs)] = 0
        inputs.append(into)
        specs.append(pl.BlockSpec(memory_space=pl.ANY))

    def body(place, *refs):
        refs = list(refs)
        step = pl.program_id(0)
        held_rows = [refs.pop(0) for _ in flat]
        shares = [refs.pop(0) for _ in range(count)] if grad else []
        if out:
            weight = refs.pop(0)
            earlier = refs.pop(0) if before is not None else None
        if aliases:
            refs.pop(0)
        rotated = jnp.concatenate([v[...] for v in held_rows], axis=0)
        if grad:
            result = refs.pop(0)
            cotangent = refs.pop(-2 if out and last else -1)

            @pl.when(step == 0)
            def _():
                parts = exchange_order([s[...] for s in shares], place[1])
                for group in range(groups):
                    start = (group % 2 * 2 + group // 2) * inner
                    for j, part in enumerate(parts):
                        to = group * held + j * inner
                        cotangent[to : to + inner, :] = part[start : start + inner]

            result[...] = (
                lax.dot_general(
                    rotated, cotangent[...], (((0,), (0,)), ((), ())), preferred_element_type=F32
                )
                * chain.scale
            )
        if out:
            total = refs.pop(-1)

            @pl.when(step == 0)
            def _():
                filled = 0 if before is None else before.shape[0]
                if filled:
                    total[:filled, :] = earlier[...]
                if filled < out * held:
                    total[filled:, :] = jnp.zeros((out * held - filled, columns), F32)

            mine = min(groups, out)
            total[(out - mine) * held :, :] += jnp.dot(
                rotated[(groups - mine) * held :], weight[...], preferred_element_type=F32
            )
            if last:

                @pl.when(step == steps - 1)
                def _():
                    for side in range(out):
                        start = side * held
                        parts = [
                            total[start + j * inner : start + (j + 1) * inner, :]
                            for j in range(count)
                        ]
                        for ref, part in zip(refs, exchange_order(parts, place[1])):
                            ref[side * inner : (side + 1) * inner, :] = part.astype(ref.dtype)

    return chain(
        body,
        inputs,
        specs,
        outs,
        out_specs,
        steps,
        scratch,
        aliases,
        flops=2 * width * columns * held * (groups * grad + out),
        late=late,
    )


def finish(chain, shares, rows, low_bits):
    rest = 1 << (low_bits - 2)

    def body(place, *refs):
        *shares, out = refs
        for position in range(1 << low_bits):
            side, middle = position // (2 * rest), position // rest % 2
            start = ((middle * 2 + side) * rest + position % rest) * rows
            here = slice(start, start + rows)
            total = shares[0][here, :]
            for other in shares[1:]:
                total = total + other[here, :].astype(F32)
            target = place[0] ^ reversed_bits(position, low_bits)
            out[pl.ds(pl.multiple_of(target * rows, rows), rows), :] = total.astype(BF16)

    tokens, columns = shares[0].shape
    tile = columns
    block = across(tokens, tile)
    (out,) = chain(
        body, shares, [block] * len(shares), [array(tokens, columns)], [block], columns // tile
    )
    return out


def per_device(activations, weight, out_grad):
    dp, tensor = lax.axis_size("dp"), lax.axis_size("tensor")
    dp_bits, top_bits = dp.bit_length() - 1, tensor.bit_length() - 1
    low_bits = dp_bits - top_bits
    rows, width = activations.shape
    me, mine = lax.axis_index("dp"), lax.axis_index("tensor")
    low_me = jnp.bitwise_and(me, (1 << low_bits) - 1)
    apart = jnp.bitwise_xor(jnp.right_shift(me, low_bits), mine)
    chain = Chain(jnp.stack([low_me, apart, mine]).astype(jnp.int32))
    chain.scale = 1.0 / math.sqrt(out_grad.shape[0] * tensor)
    factor = 1.0 / math.sqrt(width * tensor)
    rest = 1 << (low_bits - 2)
    inner = rest * rows

    def near(values, p):
        return swap(values, "dp", 1 << p)

    def core_send(blocks):
        half = len(blocks) // 2
        return [
            [kept, [near(v, 0) for v in went] if isinstance(went, list) else near(went, 0)]
            for kept, went in zip(blocks[:half], blocks[half:])
        ]

    def split_send(terms, p, *more):
        half = len(terms) // 2
        message = jnp.concatenate([add(*t).astype(BF16) for t in terms[half:]] + list(more), axis=0)
        came = near(message, p)
        pieces = [came[k * rows : (k + 1) * rows] for k in range(half + len(more))]
        kept = [t + [piece] for t, piece in zip(terms[:half], pieces)]
        return kept, pieces[half:], message

    rotation = exchange_last(activations)
    own, (ordered,) = cotangent_product(
        chain, out_grad, weight, rows, low_bits, True, 2
    )
    own = core_send(own)
    far = [swap(ordered, "tensor", q) for q in range(1, tensor)]
    half = len(own) // 2
    cut = width * 5 // 8
    sent, rotated, message, leading = rotate(
        chain, [rotation], top_bits, factor, 2, own[half:], cut
    )
    leading = near(leading, 1)
    came = near(message, 1)
    own = [terms + [came[k * rows : (k + 1) * rows]] for k, terms in enumerate(own[:half])]

    wide = list(range(2, dp_bits))
    gathered = {0: sent}
    for p in reversed(wide):
        for j in list(gathered):
            if p > 2 or j == 0:
                gathered[j | 1 << p] = near(gathered[j], p)
    gathered[0] = rotated

    others = []
    for q, grad in enumerate(far):
        late = [terms[0] for terms in own] if q == 0 else []
        products, late = cotangent_product(
            chain, grad, weight, rows, low_bits, False, 1, late
        )
        if q == 0:
            own = [[first] + terms[1:] for first, terms in zip(late, own)]
        plain = [v[0] if isinstance(v, list) else v for v in products]
        others.append(core_send(plain))

    ahead = [j for j in gathered if j and j < 1 << dp_bits and not j & 4]
    if low_bits > 2:
        own, pieces, message = split_send(own, 2, *[gathered[j] for j in ahead])
    else:
        message = jnp.concatenate([gathered[j] for j in ahead], axis=0)
        came = near(message, 2)
        pieces = [came[k * rows : (k + 1) * rows] for k in range(len(ahead))]
    gathered.update({j | 4: piece for j, piece in zip(ahead, pieces)})
    for p in range(3, low_bits):
        own, _, message = split_send(own, p)

    def gate_first(parts, after):
        held = list(chain.gate([terms[0] for part in parts for terms in part], after))
        return [[[held.pop(0)] + terms[1:] for terms in part] for part in parts]

    others = gate_first(others, [message, leading])
    others = [split_send(part, 1)[0] for part in others]

    order = [
        t << low_bits | reversed_bits(r, low_bits - 2) << 2
        for t in range(tensor)
        for r in range(rest)
    ]
    here = [gathered[j] for j in order]
    core = [near(block, 0) for block in here]
    ranges = [(0, cut), (cut, width - cut)]
    across_sent = [
        jnp.concatenate([block[:, start : start + size] for block in blocks], axis=0)
        for (start, size), blocks in zip(ranges, (here[1:], here))
    ]
    others = gate_first(others, across_sent[:1])
    messages = []
    for p in range(2, low_bits):
        sent_parts = [split_send(part, p) for part in others]
        others = [part for part, _, _ in sent_parts]
        messages = [message for _, _, message in sent_parts]
    chain.follow(across_sent[0], *messages)
    start, size = ranges[1]
    (total,) = product(chain, [here, core], [], weight, start, size, inner, out=2)
    grads = [ordered] + far
    arrived = list(chain.gate([near(across_sent[0], 1)], [total]))

    some = exchange_order([add(*part[0]) for part in [own] + others], apart)
    for p in reversed(range(top_bits)):
        count = 1 << p
        pairs = [
            (some[j], swap(some[j + count].astype(BF16), "dp", count << low_bits))
            for j in range(count)
        ]
        some = [add(*pair) for pair in pairs]
    kept, came = pairs[0]
    arrived.append(near(across_sent[1], 1))
    arrived_core = [near(arrived[0], 0)]
    leading_core = near(leading, 0)
    start, size = ranges[0]
    weight_grad, total, kept = product(
        chain, [here, core, [leading, arrived[0]], [leading_core, arrived_core[0]]], grads, weight, start, size, inner,
        before=total, grad=True, out=4, late=[kept],
    )
    (arrived[1],) = chain.gate(arrived[1:], [total])
    arrived_core.append(near(arrived[1], 0))
    rotated_grad = add(kept, came)
    final = exchange_last(rotated_grad)
    chain.follow(rotated_grad)
    start, size = ranges[1]
    result = product(
        chain, [[arrived[1]], [arrived_core[1]]], grads, weight, start, size, inner,
        before=total, out=4, last=True,
    )
    shares = [result[0]] + [swap(result[q], "tensor", q) for q in range(1, tensor)]
    held = [here, core, [arrived[1]], [arrived_core[1]]]
    part = size * 2 // 3 // LANES * LANES
    (weight_grad,) = product(
        chain, held, grads, weight, start, part, inner, into=weight_grad, grad=True, origin=start
    )
    (in_grad,) = rotate(chain, [final], top_bits, factor)
    (weight_grad,) = product(
        chain, held, grads, weight, start + part, size - part, inner, into=weight_grad, grad=True,
        origin=start,
    )
    outputs = finish(chain, shares, rows, low_bits)
    return (outputs, in_grad, weight_grad)


def solution(mesh):
    return jax.shard_map(
        per_device,
        mesh=mesh,
        in_specs=(P("dp", "tensor"), P("tensor", "dp"), P("tensor", "dp")),
        out_specs=(P("tensor", "dp"), P("dp", "tensor"), P("tensor", "dp")),
        check_vma=False,
    )
```

```python
import functools
import math

import jax
import jax.numpy as jnp
from jax import lax
from jax.experimental import pallas as pl
from jax.experimental.pallas import tpu as pltpu
from jax.sharding import PartitionSpec as P

BF16 = jnp.bfloat16
F32 = jnp.float32
VMEM_LIMIT = 67000000
LANES = 128


def swap(values, axis, mask):
    return lax.ppermute(values, axis, [(i, i ^ mask) for i in range(lax.axis_size(axis))])


def bit(number, place):
    return jnp.bitwise_and(jnp.right_shift(number, place), 1) == 1


def reversed_bits(number, count):
    return sum((number >> b & 1) << (count - 1 - b) for b in range(count))


def exchange_order(parts, apart):
    for b in range(len(parts).bit_length() - 1):
        flip = bit(apart, b)
        parts = [jnp.where(flip, parts[q ^ 1 << b], parts[q]) for q in range(len(parts))]
    return parts


class Chain:
    def __init__(self, place):
        self.place = place
        self.last = []

    def __call__(
        self,
        body,
        inputs,
        in_specs,
        outs,
        out_specs,
        steps=1,
        scratch=(),
        aliases=None,
        flops=0,
        late=(),
    ):
        count, extra = len(inputs), len(self.last)

        late = list(late)
        made = len(outs)
        skipped = count + len(late) + extra

        def kernel(place, *refs):
            body(
                place,
                *refs[:count],
                *refs[skipped : skipped + made],
                *refs[skipped + made + len(late) :],
            )

        moved = sum(math.prod(v.shape) * v.dtype.itemsize for v in list(inputs) + list(outs))
        result = pl.pallas_call(
            kernel,
            grid=(steps,),
            in_specs=[pl.BlockSpec(memory_space=pltpu.SMEM)]
            + list(in_specs)
            + [pl.BlockSpec(memory_space=pl.ANY)] * (len(late) + extra),
            out_specs=list(out_specs) + [pl.BlockSpec(memory_space=pl.ANY)] * len(late),
            scratch_shapes=list(scratch),
            out_shape=list(outs) + [jax.ShapeDtypeStruct(v.shape, v.dtype) for v in late],
            input_output_aliases={1 + k: v for k, v in (aliases or {}).items()}
            | {1 + count + k: made + k for k in range(len(late))},
            compiler_params=pltpu.CompilerParams(vmem_limit_bytes=VMEM_LIMIT),
            cost_estimate=pl.CostEstimate(flops=flops, bytes_accessed=moved, transcendentals=0),
        )(self.place, *inputs, *late, *self.last)
        self.last = [result[made - 1]]
        return result

    def gate(self, values, after):
        count = len(values)

        def body(*refs):
            del refs

        return pl.pallas_call(
            body,
            in_specs=[pl.BlockSpec(memory_space=pl.ANY)] * (count + len(after)),
            out_specs=[pl.BlockSpec(memory_space=pl.ANY)] * count,
            out_shape=[jax.ShapeDtypeStruct(v.shape, v.dtype) for v in values],
            input_output_aliases={k: k for k in range(count)},
        )(*values, *after)

    def follow(self, *values):
        self.last.extend(values)


def whole(shape):
    return pl.BlockSpec(shape, lambda i: (0,) * len(shape))


def across(rows, tile):
    return pl.BlockSpec((rows, tile), lambda i: (0, i))


def array(rows, columns, kind=BF16):
    return jax.ShapeDtypeStruct((rows, columns), kind)


def cotangent_product(chain, grad, weight, rows, low_bits, reorder, cuts=1, late=()):
    tokens, columns = grad.shape
    width = weight.shape[0]
    tile = min(2048, width)
    blocks = 1 << low_bits

    def body(place, grad, weight, *outs):
        if reorder:
            ordered = outs[-1]

            @pl.when(pl.program_id(0) == 0)
            def _():
                for position in range(blocks):
                    source = place[0] ^ reversed_bits(position, low_bits)
                    start = pl.multiple_of(source * rows, rows)
                    ordered[position * rows : (position + 1) * rows, :] = grad[
                        pl.ds(start, rows), :
                    ]

            grad = ordered
        result = lax.dot_general(
            grad[...], weight[...], (((1,), (1,)), ((), ())), preferred_element_type=F32
        ).astype(BF16)
        for position in range(plain):
            outs[position][...] = result[position * rows : (position + 1) * rows]
        for position in range(plain, blocks):
            for piece in range(cuts):
                out = outs[plain + (position - plain) * cuts + piece]

                @pl.when(pl.program_id(0) // each == piece)
                def _(out=out, position=position):
                    out[...] = result[position * rows : (position + 1) * rows]

    steps = width // tile
    cuts = min(cuts, steps)
    each = steps // cuts
    plain = blocks - blocks // 4
    count = plain + (blocks - plain) * cuts
    piece_specs = [
        pl.BlockSpec((rows, tile), lambda i, k=k: (0, jnp.clip(i - k * each, 0, each - 1)))
        for k in range(cuts)
    ]
    made = chain(
        body,
        [grad, weight],
        [whole((tokens, columns)), pl.BlockSpec((tile, columns), lambda i: (i, 0))],
        [array(rows, width)] * plain
        + [array(rows, width // cuts)] * (count - plain)
        + [array(tokens, columns)] * reorder,
        [across(rows, tile)] * plain
        + piece_specs * (blocks - plain)
        + [whole((tokens, columns))] * reorder,
        steps,
        flops=2 * tokens * width * columns,
        late=late,
    )
    pieces = [list(made[k : k + cuts]) for k in range(plain, count, cuts)]
    return list(made[:plain]) + pieces, list(made[count:])


def add(first, *others):
    total = first.astype(F32)
    for other in others:
        total = total + other.astype(F32)
    return total


def exchange_last(values):
    position = lax.axis_index("tensor")
    places = lax.axis_size("tensor").bit_length() - 1
    for place in range(places):
        sent = values.astype(BF16) if place == 0 else values
        other = swap(sent, "tensor", 1 << place)
        if place + 1 < places:
            own, other = values.astype(F32), other.astype(F32)
            values = jnp.where(bit(position, place), other - own, own + other)
    return values, other


def rotate(chain, pairs, places, factor, copies=1, sums=(), first=0):
    rows = pairs[0][0].shape[0]
    widths = [own.shape[1] for own, _ in pairs]
    width = sum(widths)
    blocks = width // LANES

    def body(place, *refs):
        ins, outs = refs[: 2 * len(pairs)], refs[len(flat) :]
        terms = list(refs[2 * len(pairs) : len(flat)])
        for k, (_, others) in enumerate(sums):
            own, start = terms.pop(0), 0
            for _ in others:
                other = terms.pop(0)
                there = slice(start, start + other.shape[1])
                total = own[:, there].astype(F32) + other[...].astype(F32)
                outs[copies][k * rows : (k + 1) * rows, there] = total.astype(BF16)
                start += other.shape[1]
        upper = bit(place[2], places - 1)
        columns = []
        for k in range(len(pairs)):
            own, other = ins[2 * k], ins[2 * k + 1]
            for start in range(0, widths[k], LANES):
                here = slice(start, start + LANES)
                a, b = own[:, here].astype(F32), other[:, here].astype(F32)
                columns.append(jnp.where(upper, b - a, a + b))
        values = jnp.concatenate(columns, axis=0)
        i = lax.broadcasted_iota(jnp.int32, (LANES, LANES), 0)
        j = lax.broadcasted_iota(jnp.int32, (LANES, LANES), 1)
        parity = i & j
        for shift in (4, 2, 1):
            parity = parity ^ (parity >> shift)
        signs = jnp.where(parity & 1 == 1, -1.0, 1.0).astype(BF16)
        high = values.astype(BF16)
        rest = values - high.astype(F32)
        middle = rest.astype(BF16)
        low = (rest - middle.astype(F32)).astype(BF16)
        result = (
            jnp.dot(low, signs, preferred_element_type=F32)
            + jnp.dot(middle, signs, preferred_element_type=F32)
        ) + jnp.dot(high, signs, preferred_element_type=F32)
        apart = 1
        while apart < blocks:
            shaped = result.reshape(blocks // (2 * apart), 2, apart * rows, LANES)
            a, b = shaped[:, 0], shaped[:, 1]
            result = jnp.stack([a + b, a - b], axis=1).reshape(blocks * rows, LANES)
            apart *= 2
        result = (result * factor).astype(BF16)
        for block in range(blocks):
            for copy in range(copies):
                outs[copy][:, block * LANES : (block + 1) * LANES] = result[
                    block * rows : (block + 1) * rows
                ]
            if block * LANES < first:
                outs[-1][:, block * LANES : (block + 1) * LANES] = result[
                    block * rows : (block + 1) * rows
                ]

    flat = [v for pair in pairs for v in pair]
    flat += [v for own, others in sums for v in [own] + list(others)]
    shapes = [(rows, width)] * copies + [(len(sums) * rows, width)] * (len(sums) > 0)
    shapes += [(rows, first)] * (first > 0)
    return chain(
        body,
        flat,
        [whole(v.shape) for v in flat],
        [array(*shape) for shape in shapes],
        [whole(shape) for shape in shapes],
        flops=6 * rows * width * LANES,
    )


def product(
    chain,
    gathered,
    grads,
    weight,
    columns_from,
    width,
    inner,
    before=None,
    into=None,
    grad=False,
    out=0,
    last=False,
    late=(),
    origin=None,
):
    features, columns = weight.shape
    origin = columns_from if origin is None else origin
    tile = math.gcd(1024, math.gcd(columns_from - origin, math.gcd(columns_from, width)))
    steps = width // tile
    first = columns_from // tile
    ahead = (columns_from - origin) // tile
    count = lax.axis_size("tensor")
    held = count * inner
    groups = len(gathered)
    flat = [v for group in gathered for v in group]
    tall = pl.BlockSpec((tile, columns), lambda i: (first + i, 0))
    share = whole((out * inner, columns))
    inputs = list(flat)
    specs = [
        pl.BlockSpec(
            (v.shape[0], tile),
            lambda i, skip=first if v.shape[1] == features else ahead: (0, skip + i),
        )
        for v in flat
    ]
    outs, out_specs, scratch, aliases = [], [], [], {}
    if grad:
        inputs += grads
        specs += [whole(v.shape) for v in grads]
        outs.append(array(features, columns, F32))
        out_specs.append(tall)
        scratch.append(pltpu.VMEM((groups * held, columns), BF16))
    if out:
        square = whole((out * held, columns))
        inputs.append(weight)
        specs.append(tall)
        if before is not None:
            inputs.append(before)
            specs.append(whole(before.shape))
        if last:
            outs += [array(out * inner, columns, F32)] + [array(out * inner, columns)] * (count - 1)
            out_specs += [share] * count
            scratch.append(pltpu.VMEM((out * held, columns), F32))
        else:
            outs.append(array(out * held, columns, F32))
            out_specs.append(square)
    if into is not None:
        aliases[len(inputs)] = 0
        inputs.append(into)
        specs.append(pl.BlockSpec(memory_space=pl.ANY))

    def body(place, *refs):
        refs = list(refs)
        step = pl.program_id(0)
        held_rows = [refs.pop(0) for _ in flat]
        shares = [refs.pop(0) for _ in range(count)] if grad else []
        if out:
            weight = refs.pop(0)
            earlier = refs.pop(0) if before is not None else None
        if aliases:
            refs.pop(0)
        rotated = jnp.concatenate([v[...] for v in held_rows], axis=0)
        if grad:
            result = refs.pop(0)
            cotangent = refs.pop(-2 if out and last else -1)

            @pl.when(step == 0)
            def _():
                parts = exchange_order([s[...] for s in shares], place[1])
                for group in range(groups):
                    start = (group % 2 * 2 + group // 2) * inner
                    for j, part in enumerate(parts):
                        to = group * held + j * inner
                        cotangent[to : to + inner, :] = part[start : start + inner]

            result[...] = (
                lax.dot_general(
                    rotated, cotangent[...], (((0,), (0,)), ((), ())), preferred_element_type=F32
                )
                * chain.scale
            )
        if out:
            total = refs.pop(-1)

            @pl.when(step == 0)
            def _():
                filled = 0 if before is None else before.shape[0]
                if filled:
                    total[:filled, :] = earlier[...]
                if filled < out * held:
                    total[filled:, :] = jnp.zeros((out * held - filled, columns), F32)

            mine = min(groups, out)
            total[(out - mine) * held :, :] += jnp.dot(
                rotated[(groups - mine) * held :], weight[...], preferred_element_type=F32
            )
            if last:

                @pl.when(step == steps - 1)
                def _():
                    for side in range(out):
                        start = side * held
                        parts = [
                            total[start + j * inner : start + (j + 1) * inner, :]
                            for j in range(count)
                        ]
                        for ref, part in zip(refs, exchange_order(parts, place[1])):
                            ref[side * inner : (side + 1) * inner, :] = part.astype(ref.dtype)

    return chain(
        body,
        inputs,
        specs,
        outs,
        out_specs,
        steps,
        scratch,
        aliases,
        flops=2 * width * columns * held * (groups * grad + out),
        late=late,
    )


def finish(chain, parts, rows, low_bits):
    each = len(parts[0])
    rest = 1 << (low_bits - 2)

    def body(place, *refs):
        *shares, out = refs
        for position in range(1 << low_bits):
            side, middle = position // (2 * rest), position // rest % 2
            start = (side * rest + position % rest) * rows
            here = slice(start, start + rows)
            total = shares[middle * each][here, :]
            for other in shares[middle * each + 1 : (middle + 1) * each]:
                total = total + other[here, :].astype(F32)
            target = place[0] ^ reversed_bits(position, low_bits)
            out[pl.ds(pl.multiple_of(target * rows, rows), rows), :] = total.astype(BF16)

    flat = [v for part in parts for v in part]
    shape = (rows << low_bits, flat[0].shape[1])
    (out,) = chain(body, flat, [whole(v.shape) for v in flat], [array(*shape)], [whole(shape)])
    return out


def per_device(activations, weight, out_grad):
    dp, tensor = lax.axis_size("dp"), lax.axis_size("tensor")
    dp_bits, top_bits = dp.bit_length() - 1, tensor.bit_length() - 1
    low_bits = dp_bits - top_bits
    rows, width = activations.shape
    me, mine = lax.axis_index("dp"), lax.axis_index("tensor")
    low_me = jnp.bitwise_and(me, (1 << low_bits) - 1)
    apart = jnp.bitwise_xor(jnp.right_shift(me, low_bits), mine)
    chain = Chain(jnp.stack([low_me, apart, mine]).astype(jnp.int32))
    chain.scale = 1.0 / math.sqrt(out_grad.shape[0] * tensor)
    factor = 1.0 / math.sqrt(width * tensor)
    rest = 1 << (low_bits - 2)
    inner = rest * rows

    def near(values, p):
        return swap(values, "dp", 1 << p)

    def core_send(blocks):
        half = len(blocks) // 2
        return [
            [kept, [near(v, 0) for v in went] if isinstance(went, list) else near(went, 0)]
            for kept, went in zip(blocks[:half], blocks[half:])
        ]

    def split_send(terms, p, *more):
        half = len(terms) // 2
        message = jnp.concatenate([add(*t).astype(BF16) for t in terms[half:]] + list(more), axis=0)
        came = near(message, p)
        pieces = [came[k * rows : (k + 1) * rows] for k in range(half + len(more))]
        kept = [t + [piece] for t, piece in zip(terms[:half], pieces)]
        return kept, pieces[half:], message

    rotation = exchange_last(activations)
    own, (ordered,) = cotangent_product(
        chain, out_grad, weight, rows, low_bits, True, 2
    )
    own = core_send(own)
    far = [swap(ordered, "tensor", q) for q in range(1, tensor)]
    half = len(own) // 2
    cut = width * 5 // 8
    sent, rotated, message, leading = rotate(
        chain, [rotation], top_bits, factor, 2, own[half:], cut
    )
    leading = near(leading, 1)
    came = near(message, 1)
    own = [terms + [came[k * rows : (k + 1) * rows]] for k, terms in enumerate(own[:half])]

    wide = list(range(2, dp_bits))
    gathered = {0: sent}
    for p in reversed(wide):
        for j in list(gathered):
            if p > 2 or j == 0:
                gathered[j | 1 << p] = near(gathered[j], p)
    gathered[0] = rotated

    others = []
    for q, grad in enumerate(far):
        late = [terms[0] for terms in own] if q == 0 else []
        products, late = cotangent_product(
            chain, grad, weight, rows, low_bits, False, 1, late
        )
        if q == 0:
            own = [[first] + terms[1:] for first, terms in zip(late, own)]
        plain = [v[0] if isinstance(v, list) else v for v in products]
        others.append(core_send(plain))

    ahead = [j for j in gathered if j and j < 1 << dp_bits and not j & 4]
    if low_bits > 2:
        own, pieces, message = split_send(own, 2, *[gathered[j] for j in ahead])
    else:
        message = jnp.concatenate([gathered[j] for j in ahead], axis=0)
        came = near(message, 2)
        pieces = [came[k * rows : (k + 1) * rows] for k in range(len(ahead))]
    gathered.update({j | 4: piece for j, piece in zip(ahead, pieces)})
    for p in range(3, low_bits):
        own, _, message = split_send(own, p)

    def gate_first(parts, after):
        held = list(chain.gate([terms[0] for part in parts for terms in part], after))
        return [[[held.pop(0)] + terms[1:] for terms in part] for part in parts]

    others = gate_first(others, [message, leading])
    others = [split_send(part, 1)[0] for part in others]

    order = [
        t << low_bits | reversed_bits(r, low_bits - 2) << 2
        for t in range(tensor)
        for r in range(rest)
    ]
    here = [gathered[j] for j in order]
    core = [near(block, 0) for block in here]
    ranges = [(0, cut), (cut, width - cut)]
    across_sent = [
        jnp.concatenate([block[:, start : start + size] for block in blocks], axis=0)
        for (start, size), blocks in zip(ranges, (here[1:], here))
    ]
    others = gate_first(others, across_sent[:1])
    messages = []
    for p in range(2, low_bits):
        sent_parts = [split_send(part, p) for part in others]
        others = [part for part, _, _ in sent_parts]
        messages = [message for _, _, message in sent_parts]
    chain.follow(across_sent[0], *messages)
    total, *early = product(chain, [here, core], [], weight, 0, width, inner, out=2, last=True)
    early = [total] + [swap(early[q - 1], "tensor", q) for q in range(1, tensor)]
    grads = [ordered] + far
    arrived = list(chain.gate([near(across_sent[0], 1)], [total]))

    some = exchange_order([add(*part[0]) for part in [own] + others], apart)
    for p in reversed(range(top_bits)):
        count = 1 << p
        pairs = [
            (some[j], swap(some[j + count].astype(BF16), "dp", count << low_bits))
            for j in range(count)
        ]
        some = [add(*pair) for pair in pairs]
    kept, came = pairs[0]
    arrived.append(near(across_sent[1], 1))
    arrived_core = [near(arrived[0], 0)]
    leading_core = near(leading, 0)
    start, size = ranges[0]
    weight_grad, total, kept = product(
        chain, [here, core, [leading, arrived[0]], [leading_core, arrived_core[0]]], grads, weight, start, size, inner,
        grad=True, out=2, late=[kept],
    )
    (arrived[1],) = chain.gate(arrived[1:], [total])
    arrived_core.append(near(arrived[1], 0))
    rotated_grad = add(kept, came)
    final = exchange_last(rotated_grad)
    chain.follow(rotated_grad, *early[1:])
    start, size = ranges[1]
    result = product(
        chain, [[arrived[1]], [arrived_core[1]]], grads, weight, start, size, inner,
        before=total, out=2, last=True,
    )
    shares = [result[0]] + [swap(result[q], "tensor", q) for q in range(1, tensor)]
    held = [here, core, [arrived[1]], [arrived_core[1]]]
    part = size * 2 // 3 // LANES * LANES
    (weight_grad,) = product(
        chain, held, grads, weight, start, part, inner, into=weight_grad, grad=True, origin=start
    )
    (in_grad,) = rotate(chain, [final], top_bits, factor)
    (weight_grad,) = product(
        chain, held, grads, weight, start + part, size - part, inner, into=weight_grad, grad=True,
        origin=start,
    )
    outputs = finish(chain, [early, shares], rows, low_bits)
    return (outputs, in_grad, weight_grad)


def solution(mesh):
    return jax.shard_map(
        per_device,
        mesh=mesh,
        in_specs=(P("dp", "tensor"), P("tensor", "dp"), P("tensor", "dp")),
        out_specs=(P("tensor", "dp"), P("dp", "tensor"), P("tensor", "dp")),
        check_vma=False,
    )
```

```python
import functools
import math

import jax
import jax.numpy as jnp
from jax import lax
from jax.experimental import pallas as pl
from jax.experimental.pallas import tpu as pltpu
from jax.sharding import PartitionSpec as P

BF16 = jnp.bfloat16
F32 = jnp.float32
VMEM_LIMIT = 67000000
LANES = 128


def swap(values, axis, mask):
    return lax.ppermute(values, axis, [(i, i ^ mask) for i in range(lax.axis_size(axis))])


def bit(number, place):
    return jnp.bitwise_and(jnp.right_shift(number, place), 1) == 1


def reversed_bits(number, count):
    return sum((number >> b & 1) << (count - 1 - b) for b in range(count))


def exchange_order(parts, apart):
    for b in range(len(parts).bit_length() - 1):
        flip = bit(apart, b)
        parts = [jnp.where(flip, parts[q ^ 1 << b], parts[q]) for q in range(len(parts))]
    return parts


class Chain:
    def __init__(self, place):
        self.place = place
        self.last = []

    def __call__(
        self,
        body,
        inputs,
        in_specs,
        outs,
        out_specs,
        steps=1,
        scratch=(),
        aliases=None,
        flops=0,
        late=(),
    ):
        count, extra = len(inputs), len(self.last)

        late = list(late)
        made = len(outs)
        skipped = count + len(late) + extra

        def kernel(place, *refs):
            body(
                place,
                *refs[:count],
                *refs[skipped : skipped + made],
                *refs[skipped + made + len(late) :],
            )

        moved = sum(math.prod(v.shape) * v.dtype.itemsize for v in list(inputs) + list(outs))
        result = pl.pallas_call(
            kernel,
            grid=(steps,),
            in_specs=[pl.BlockSpec(memory_space=pltpu.SMEM)]
            + list(in_specs)
            + [pl.BlockSpec(memory_space=pl.ANY)] * (len(late) + extra),
            out_specs=list(out_specs) + [pl.BlockSpec(memory_space=pl.ANY)] * len(late),
            scratch_shapes=list(scratch),
            out_shape=list(outs) + [jax.ShapeDtypeStruct(v.shape, v.dtype) for v in late],
            input_output_aliases={1 + k: v for k, v in (aliases or {}).items()}
            | {1 + count + k: made + k for k in range(len(late))},
            compiler_params=pltpu.CompilerParams(vmem_limit_bytes=VMEM_LIMIT),
            cost_estimate=pl.CostEstimate(flops=flops, bytes_accessed=moved, transcendentals=0),
        )(self.place, *inputs, *late, *self.last)
        self.last = [result[made - 1]]
        return result

    def gate(self, values, after):
        count = len(values)

        def body(*refs):
            del refs

        return pl.pallas_call(
            body,
            in_specs=[pl.BlockSpec(memory_space=pl.ANY)] * (count + len(after)),
            out_specs=[pl.BlockSpec(memory_space=pl.ANY)] * count,
            out_shape=[jax.ShapeDtypeStruct(v.shape, v.dtype) for v in values],
            input_output_aliases={k: k for k in range(count)},
        )(*values, *after)

    def follow(self, *values):
        self.last.extend(values)


def whole(shape):
    return pl.BlockSpec(shape, lambda i: (0,) * len(shape))


def across(rows, tile):
    return pl.BlockSpec((rows, tile), lambda i: (0, i))


def array(rows, columns, kind=BF16):
    return jax.ShapeDtypeStruct((rows, columns), kind)


def cotangent_product(chain, grad, weight, rows, low_bits, reorder, cuts=1, late=()):
    tokens, columns = grad.shape
    width = weight.shape[0]
    tile = min(2048, width)
    blocks = 1 << low_bits

    def body(place, grad, weight, *outs):
        if reorder:
            ordered = outs[-1]

            @pl.when(pl.program_id(0) == 0)
            def _():
                for position in range(blocks):
                    source = place[0] ^ reversed_bits(position, low_bits)
                    start = pl.multiple_of(source * rows, rows)
                    ordered[position * rows : (position + 1) * rows, :] = grad[
                        pl.ds(start, rows), :
                    ]

            grad = ordered
        result = lax.dot_general(
            grad[...], weight[...], (((1,), (1,)), ((), ())), preferred_element_type=F32
        ).astype(BF16)
        for position in range(plain):
            outs[position][...] = result[position * rows : (position + 1) * rows]
        for position in range(plain, blocks):
            for piece in range(cuts):
                out = outs[plain + (position - plain) * cuts + piece]

                @pl.when(pl.program_id(0) // each == piece)
                def _(out=out, position=position):
                    out[...] = result[position * rows : (position + 1) * rows]

    steps = width // tile
    cuts = min(cuts, steps)
    each = steps // cuts
    plain = blocks - blocks // 4
    count = plain + (blocks - plain) * cuts
    piece_specs = [
        pl.BlockSpec((rows, tile), lambda i, k=k: (0, jnp.clip(i - k * each, 0, each - 1)))
        for k in range(cuts)
    ]
    made = chain(
        body,
        [grad, weight],
        [whole((tokens, columns)), pl.BlockSpec((tile, columns), lambda i: (i, 0))],
        [array(rows, width)] * plain
        + [array(rows, width // cuts)] * (count - plain)
        + [array(tokens, columns)] * reorder,
        [across(rows, tile)] * plain
        + piece_specs * (blocks - plain)
        + [whole((tokens, columns))] * reorder,
        steps,
        flops=2 * tokens * width * columns,
        late=late,
    )
    pieces = [list(made[k : k + cuts]) for k in range(plain, count, cuts)]
    return list(made[:plain]) + pieces, list(made[count:])


def add(first, *others):
    total = first.astype(F32)
    for other in others:
        total = total + other.astype(F32)
    return total


def exchange_last(values):
    position = lax.axis_index("tensor")
    places = lax.axis_size("tensor").bit_length() - 1
    for place in range(places):
        sent = values.astype(BF16) if place == 0 else values
        other = swap(sent, "tensor", 1 << place)
        if place + 1 < places:
            own, other = values.astype(F32), other.astype(F32)
            values = jnp.where(bit(position, place), other - own, own + other)
    return values, other


def rotate(chain, pairs, places, factor, copies=1, sums=(), first=0):
    rows = pairs[0][0].shape[0]
    widths = [own.shape[1] for own, _ in pairs]
    width = sum(widths)
    blocks = width // LANES

    def body(place, *refs):
        ins, outs = refs[: 2 * len(pairs)], refs[len(flat) :]
        terms = list(refs[2 * len(pairs) : len(flat)])
        for k, (_, others) in enumerate(sums):
            own, start = terms.pop(0), 0
            for _ in others:
                other = terms.pop(0)
                there = slice(start, start + other.shape[1])
                total = own[:, there].astype(F32) + other[...].astype(F32)
                outs[copies][k * rows : (k + 1) * rows, there] = total.astype(BF16)
                start += other.shape[1]
        upper = bit(place[2], places - 1)
        columns = []
        for k in range(len(pairs)):
            own, other = ins[2 * k], ins[2 * k + 1]
            for start in range(0, widths[k], LANES):
                here = slice(start, start + LANES)
                a, b = own[:, here].astype(F32), other[:, here].astype(F32)
                columns.append(jnp.where(upper, b - a, a + b))
        values = jnp.concatenate(columns, axis=0)
        i = lax.broadcasted_iota(jnp.int32, (LANES, LANES), 0)
        j = lax.broadcasted_iota(jnp.int32, (LANES, LANES), 1)
        parity = i & j
        for shift in (4, 2, 1):
            parity = parity ^ (parity >> shift)
        signs = jnp.where(parity & 1 == 1, -1.0, 1.0).astype(BF16)
        high = values.astype(BF16)
        rest = values - high.astype(F32)
        middle = rest.astype(BF16)
        low = (rest - middle.astype(F32)).astype(BF16)
        result = (
            jnp.dot(low, signs, preferred_element_type=F32)
            + jnp.dot(middle, signs, preferred_element_type=F32)
        ) + jnp.dot(high, signs, preferred_element_type=F32)
        apart = 1
        while apart < blocks:
            shaped = result.reshape(blocks // (2 * apart), 2, apart * rows, LANES)
            a, b = shaped[:, 0], shaped[:, 1]
            result = jnp.stack([a + b, a - b], axis=1).reshape(blocks * rows, LANES)
            apart *= 2
        result = (result * factor).astype(BF16)
        for block in range(blocks):
            for copy in range(copies):
                outs[copy][:, block * LANES : (block + 1) * LANES] = result[
                    block * rows : (block + 1) * rows
                ]
            if block * LANES < first:
                outs[-1][:, block * LANES : (block + 1) * LANES] = result[
                    block * rows : (block + 1) * rows
                ]

    flat = [v for pair in pairs for v in pair]
    flat += [v for own, others in sums for v in [own] + list(others)]
    shapes = [(rows, width)] * copies + [(len(sums) * rows, width)] * (len(sums) > 0)
    shapes += [(rows, first)] * (first > 0)
    return chain(
        body,
        flat,
        [whole(v.shape) for v in flat],
        [array(*shape) for shape in shapes],
        [whole(shape) for shape in shapes],
        flops=6 * rows * width * LANES,
    )


def product(
    chain,
    gathered,
    grads,
    weight,
    columns_from,
    width,
    inner,
    before=None,
    into=None,
    grad=False,
    out=0,
    last=False,
    late=(),
    origin=None,
):
    features, columns = weight.shape
    origin = columns_from if origin is None else origin
    tile = math.gcd(1024, math.gcd(columns_from - origin, math.gcd(columns_from, width)))
    steps = width // tile
    first = columns_from // tile
    ahead = (columns_from - origin) // tile
    count = lax.axis_size("tensor")
    held = count * inner
    groups = len(gathered)
    flat = [v for group in gathered for v in group]
    tall = pl.BlockSpec((tile, columns), lambda i: (first + i, 0))
    share = whole((out * inner, columns))
    inputs = list(flat)
    specs = [
        pl.BlockSpec(
            (v.shape[0], tile),
            lambda i, skip=first if v.shape[1] == features else ahead: (0, skip + i),
        )
        for v in flat
    ]
    outs, out_specs, scratch, aliases = [], [], [], {}
    if grad:
        inputs += grads
        specs += [whole(v.shape) for v in grads]
        outs.append(array(features, columns, F32))
        out_specs.append(tall)
        scratch.append(pltpu.VMEM((groups * held, columns), BF16))
    if out:
        square = whole((out * held, columns))
        inputs.append(weight)
        specs.append(tall)
        if before is not None:
            inputs.append(before)
            specs.append(whole(before.shape))
        if last:
            outs += [array(out * inner, columns, F32)] + [array(out * inner, columns)] * (count - 1)
            out_specs += [share] * count
            scratch.append(pltpu.VMEM((out * held, columns), F32))
        else:
            outs.append(array(out * held, columns, F32))
            out_specs.append(square)
    if into is not None:
        aliases[len(inputs)] = 0
        inputs.append(into)
        specs.append(pl.BlockSpec(memory_space=pl.ANY))

    def body(place, *refs):
        refs = list(refs)
        step = pl.program_id(0)
        held_rows = [refs.pop(0) for _ in flat]
        shares = [refs.pop(0) for _ in range(count)] if grad else []
        if out:
            weight = refs.pop(0)
            earlier = refs.pop(0) if before is not None else None
        if aliases:
            refs.pop(0)
        rotated = jnp.concatenate([v[...] for v in held_rows], axis=0)
        if grad:
            result = refs.pop(0)
            cotangent = refs.pop(-2 if out and last else -1)

            @pl.when(step == 0)
            def _():
                parts = exchange_order([s[...] for s in shares], place[1])
                for group in range(groups):
                    start = (group % 2 * 2 + group // 2) * inner
                    for j, part in enumerate(parts):
                        to = group * held + j * inner
                        cotangent[to : to + inner, :] = part[start : start + inner]

            result[...] = (
                lax.dot_general(
                    rotated, cotangent[...], (((0,), (0,)), ((), ())), preferred_element_type=F32
                )
                * chain.scale
            )
        if out:
            total = refs.pop(-1)

            @pl.when(step == 0)
            def _():
                filled = 0 if before is None else before.shape[0]
                if filled:
                    total[:filled, :] = earlier[...]
                if filled < out * held:
                    total[filled:, :] = jnp.zeros((out * held - filled, columns), F32)

            mine = min(groups, out)
            total[(out - mine) * held :, :] += jnp.dot(
                rotated[(groups - mine) * held :], weight[...], preferred_element_type=F32
            )
            if last:

                @pl.when(step == steps - 1)
                def _():
                    for side in range(out):
                        start = side * held
                        parts = [
                            total[start + j * inner : start + (j + 1) * inner, :]
                            for j in range(count)
                        ]
                        for ref, part in zip(refs, exchange_order(parts, place[1])):
                            ref[side * inner : (side + 1) * inner, :] = part.astype(ref.dtype)

    return chain(
        body,
        inputs,
        specs,
        outs,
        out_specs,
        steps,
        scratch,
        aliases,
        flops=2 * width * columns * held * (groups * grad + out),
        late=late,
    )


def finish(chain, parts, rows, low_bits):
    each = len(parts[0])
    rest = 1 << (low_bits - 2)

    def body(place, *refs):
        *shares, out = refs
        for position in range(1 << low_bits):
            side, middle = position // (2 * rest), position // rest % 2
            start = (side * rest + position % rest) * rows
            here = slice(start, start + rows)
            total = shares[middle * each][here, :]
            for other in shares[middle * each + 1 : (middle + 1) * each]:
                total = total + other[here, :].astype(F32)
            target = place[0] ^ reversed_bits(position, low_bits)
            out[pl.ds(pl.multiple_of(target * rows, rows), rows), :] = total.astype(BF16)

    flat = [v for part in parts for v in part]
    shape = (rows << low_bits, flat[0].shape[1])
    (out,) = chain(body, flat, [whole(v.shape) for v in flat], [array(*shape)], [whole(shape)])
    return out


def per_device(activations, weight, out_grad):
    dp, tensor = lax.axis_size("dp"), lax.axis_size("tensor")
    dp_bits, top_bits = dp.bit_length() - 1, tensor.bit_length() - 1
    low_bits = dp_bits - top_bits
    rows, width = activations.shape
    me, mine = lax.axis_index("dp"), lax.axis_index("tensor")
    low_me = jnp.bitwise_and(me, (1 << low_bits) - 1)
    apart = jnp.bitwise_xor(jnp.right_shift(me, low_bits), mine)
    chain = Chain(jnp.stack([low_me, apart, mine]).astype(jnp.int32))
    chain.scale = 1.0 / math.sqrt(out_grad.shape[0] * tensor)
    factor = 1.0 / math.sqrt(width * tensor)
    rest = 1 << (low_bits - 2)
    inner = rest * rows

    def near(values, p):
        return swap(values, "dp", 1 << p)

    def core_send(blocks):
        half = len(blocks) // 2
        return [
            [kept, [near(v, 0) for v in went] if isinstance(went, list) else near(went, 0)]
            for kept, went in zip(blocks[:half], blocks[half:])
        ]

    def split_send(terms, p, *more):
        half = len(terms) // 2
        message = jnp.concatenate([add(*t).astype(BF16) for t in terms[half:]] + list(more), axis=0)
        came = near(message, p)
        pieces = [came[k * rows : (k + 1) * rows] for k in range(half + len(more))]
        kept = [t + [piece] for t, piece in zip(terms[:half], pieces)]
        return kept, pieces[half:], message

    rotation = exchange_last(activations)
    own, (ordered,) = cotangent_product(
        chain, out_grad, weight, rows, low_bits, True, 2
    )
    own = core_send(own)
    far = [swap(ordered, "tensor", q) for q in range(1, tensor)]
    half = len(own) // 2
    cut = width * 5 // 8
    sent, rotated, message, leading = rotate(
        chain, [rotation], top_bits, factor, 2, own[half:], cut
    )
    leading = near(leading, 1)
    came = near(message, 1)
    own = [terms + [came[k * rows : (k + 1) * rows]] for k, terms in enumerate(own[:half])]

    wide = list(range(2, dp_bits))
    gathered = {0: sent}
    for p in reversed(wide):
        for j in list(gathered):
            if p > 2 or j == 0:
                gathered[j | 1 << p] = near(gathered[j], p)
    gathered[0] = rotated

    others = []
    for q, grad in enumerate(far):
        late = [terms[0] for terms in own] if q == 0 else []
        products, late = cotangent_product(
            chain, grad, weight, rows, low_bits, False, 1, late
        )
        if q == 0:
            own = [[first] + terms[1:] for first, terms in zip(late, own)]
        plain = [v[0] if isinstance(v, list) else v for v in products]
        others.append(core_send(plain))

    ahead = [j for j in gathered if j and j < 1 << dp_bits and not j & 4]
    if low_bits > 2:
        own, pieces, message = split_send(own, 2, *[gathered[j] for j in ahead])
    else:
        message = jnp.concatenate([gathered[j] for j in ahead], axis=0)
        came = near(message, 2)
        pieces = [came[k * rows : (k + 1) * rows] for k in range(len(ahead))]
    gathered.update({j | 4: piece for j, piece in zip(ahead, pieces)})
    for p in range(3, low_bits):
        own, _, message = split_send(own, p)

    def gate_first(parts, after):
        held = list(chain.gate([terms[0] for part in parts for terms in part], after))
        return [[[held.pop(0)] + terms[1:] for terms in part] for part in parts]

    others = gate_first(others, [message, leading])
    others = [split_send(part, 1)[0] for part in others]

    order = [
        t << low_bits | reversed_bits(r, low_bits - 2) << 2
        for t in range(tensor)
        for r in range(rest)
    ]
    here = [gathered[j] for j in order]
    core = [near(block, 0) for block in here]
    ranges = [(0, cut), (cut, width - cut)]
    across_sent = [
        jnp.concatenate([block[:, start : start + size] for block in blocks], axis=0)
        for (start, size), blocks in zip(ranges, (here[1:], here))
    ]
    others = gate_first(others, across_sent[:1])
    messages = []
    for p in range(2, low_bits):
        sent_parts = [split_send(part, p) for part in others]
        others = [part for part, _, _ in sent_parts]
        messages = [message for _, _, message in sent_parts]
    chain.follow(across_sent[0], *messages)
    total, *early = product(chain, [here, core], [], weight, 0, width, inner, out=2, last=True)
    early = [total] + [swap(early[q - 1], "tensor", q) for q in range(1, tensor)]
    grads = [ordered] + far
    arrived = list(chain.gate([near(across_sent[0], 1)], [total]))

    some = exchange_order([add(*part[0]) for part in [own] + others], apart)
    for p in reversed(range(top_bits)):
        count = 1 << p
        pairs = [
            (some[j], swap(some[j + count].astype(BF16), "dp", count << low_bits))
            for j in range(count)
        ]
        some = [add(*pair) for pair in pairs]
    kept, came = pairs[0]
    arrived.append(near(across_sent[1], 1))
    arrived_core = [near(arrived[0], 0)]
    leading_core = near(leading, 0)
    start, size = ranges[0]
    weight_grad, total, kept = product(
        chain, [here, core, [leading, arrived[0]], [leading_core, arrived_core[0]]], grads, weight, start, size, inner,
        grad=True, out=2, late=[kept],
    )
    (arrived[1],) = chain.gate(arrived[1:], [total])
    arrived_core.append(near(arrived[1], 0))
    rotated_grad = add(kept, came)
    final = exchange_last(rotated_grad)
    chain.follow(rotated_grad, *early[1:])
    start, size = ranges[1]
    result = product(
        chain, [[arrived[1]], [arrived_core[1]]], grads, weight, start, size, inner,
        before=total, out=2, last=True,
    )
    shares = [result[0]] + [swap(result[q], "tensor", q) for q in range(1, tensor)]
    held = [here, core, [arrived[1]], [arrived_core[1]]]
    (weight_grad,) = product(
        chain, held, grads, weight, start, size, inner, into=weight_grad, grad=True
    )
    (in_grad,) = rotate(chain, [final], top_bits, factor)
    outputs = finish(chain, [early, shares], rows, low_bits)
    return (outputs, in_grad, weight_grad)


def solution(mesh):
    return jax.shard_map(
        per_device,
        mesh=mesh,
        in_specs=(P("dp", "tensor"), P("tensor", "dp"), P("tensor", "dp")),
        out_specs=(P("tensor", "dp"), P("dp", "tensor"), P("tensor", "dp")),
        check_vma=False,
    )
```
